256 devices in a mesh: species: 8 (over x, y_hi), ctx: 32 (over y_lo, z, core).
Axes of the slice: x: 4, y: 4 (y_hi: 2, y_lo: 2; y = y_hi * 2 + y_lo), z: 8, core: 2. Of those that a mesh axis runs over, the one named last changes fastest.
Arguments:
- tokens: bfloat16 [8, 16384, 1024], P('species', 'ctx'), may hold values from -6 to 6
- gap_mask: int32 [8, 32], replicated, may hold values from 0 to 1, as said below
- window_reach: int32 [32], replicated, may hold values from 128 to 512
- row_qkv: bfloat16 [1024, 1536], replicated
- row_out: bfloat16 [512, 1024], replicated, may hold values from -3 to 3
- col_qkv: bfloat16 [1024, 1536], replicated
- col_out: bfloat16 [512, 1024], replicated, may hold values from -0.5 to 0.5
Outputs:
- mixed: bfloat16 [8, 16384, 1024], P('species', 'ctx')
The draws below stay inside these ranges and needn't reach their ends.
Inputs may be any that keep to these rules, and one draw needn't show every extreme that they name: `gap_mask`: species row 0 is 1 in every block.
All inputs are finite; a program needn't handle non-finite values.
Results may differ from the reference program's by a relative error of at most 0.015.
Values may be sent and summed in bfloat16 or wider, within the bound.
No kernel may reach another device: no remote copies, remote signals or barrier semaphores. Data moves between devices by JAX's collectives and lax.ppermute only.
A program may use at most 128 MiB of HBM per device.

```python
import jax
import jax.numpy as jnp
from jax import lax

D = 1024
HEADS = 8
HEAD = 64
BLOCK = 512
HD = 512
SPECIES = 8
NBLK = 32
COLS = 16384


def projection_matrix(key):
    return jax.random.normal(key, (D, 3 * HD), jnp.float32) * D ** (-0.5)


def draw_gap_mask(key, part):
    key = jax.random.fold_in(key, 1)
    marks = (jax.random.randint(key, (SPECIES, NBLK), 0, 10) < 7).astype(jnp.int32)
    return marks.at[0].set(1)


def draw_window_reach(key, part):
    key = jax.random.fold_in(key, 2)
    first_key, second_key = jax.random.split(key)
    reach_all = jax.random.randint(first_key, (NBLK,), BLOCK // 4, BLOCK + 1)
    chosen = jax.random.randint(second_key, (), 0, NBLK)
    return reach_all.at[chosen].set(BLOCK).astype(jnp.int32)


def draw_row_qkv(key, part):
    key = jax.random.fold_in(key, 3)
    matrix = projection_matrix(key)
    return matrix.astype(jnp.bfloat16)


def draw_col_qkv(key, part):
    key = jax.random.fold_in(key, 4)
    matrix = projection_matrix(key)
    return matrix.astype(jnp.bfloat16)


def block_levels(key, dims, cuts, smallest, largest):
    gain, own = 1.0, jax.random.fold_in(key, 6)
    for dim, parts in cuts:
        steps = jnp.exp(jax.random.uniform(jax.random.fold_in(own, dim), (parts,), jnp.float32, smallest / len(cuts), largest / len(cuts)))
        gain = gain * jnp.repeat(steps, dims[dim] // parts).reshape([-1 if axis == dim else 1 for axis in range(len(dims))])
    return gain


def bell_draw(key, extent, scale, limit, pieces=(), held_as=jnp.bfloat16):
    values = jax.random.normal(key, extent, jnp.float32) * scale
    if len(pieces) > 0:
        values = block_levels(key, extent, pieces, -0.22, 0.18) * values
    return jnp.clip(values, min=-limit, max=limit).astype(held_as)


def setup_inputs(seed: int = 0) -> dict:
    seeds = jax.random.split(jax.random.key(seed), 8)
    return {
        "tokens": bell_draw(seeds[0], (SPECIES, COLS, D), 1.0, 6.0, ((0, 8), (1, 32))),
        "gap_mask": draw_gap_mask(jax.random.fold_in(seeds[7], 71), 0),
        "window_reach": draw_window_reach(jax.random.fold_in(seeds[7], 71), 0),
        "row_qkv": draw_row_qkv(jax.random.fold_in(seeds[7], 71), 0),
        "row_out": bell_draw(seeds[4], (HD, D), 4 ** -0.5, 3.0),
        "col_qkv": draw_col_qkv(jax.random.fold_in(seeds[7], 71), 0),
        "col_out": bell_draw(seeds[6], (HD, D), 128 ** -0.5, 0.5),
    }


def rms_rows(values):
    return values * lax.rsqrt(lax.optimization_barrier(jnp.mean(values * values, axis=-1, keepdims=True)) + 1e-06)

def softmax_last(scores):
    maxima = lax.optimization_barrier(jnp.max(scores, axis=-1, keepdims=True))
    expsum = jnp.exp(scores - maxima)
    return expsum / lax.optimization_barrier(jnp.sum(expsum, axis=-1, keepdims=True))

def row_attend(queries, keyval, usable):
    blocklen = queries.shape[0]
    keylen = keyval.shape[0]
    query_heads = queries.astype(jnp.float32).reshape(blocklen, HEADS, HEAD)
    key_heads = keyval[:, :HD].astype(jnp.float32).reshape(keylen, HEADS, HEAD)
    value_heads = keyval[:, HD:].astype(jnp.float32).reshape(keylen, HEADS, HEAD)
    scores = jnp.einsum('qhd,khd->hqk', query_heads, key_heads) * HEAD ** (-0.5)
    scores = jnp.where(usable[None, None, :], scores, -1e+30)
    weights = softmax_last(scores).astype(jnp.bfloat16)
    attended = jnp.einsum('hqk,khd->qhd', weights.astype(jnp.float32), value_heads)
    return attended.astype(jnp.bfloat16).reshape(blocklen, HD)

def column_attend(queries, keyval, alive):
    query_count, columns, _ = queries.shape
    key_count = keyval.shape[0]
    query_heads = queries.astype(jnp.float32).reshape(query_count, columns, HEADS, HEAD)
    key_heads = keyval[..., :HD].astype(jnp.float32).reshape(key_count, columns, HEADS, HEAD)
    value_heads = keyval[..., HD:].astype(jnp.float32).reshape(key_count, columns, HEADS, HEAD)
    scores = jnp.einsum('schd,tchd->hsct', query_heads, key_heads) * HEAD ** (-0.5)
    scores = jnp.where(alive[None, None, None, :], scores, -1e+30)
    weights = softmax_last(scores).astype(jnp.bfloat16)
    attended = jnp.einsum('hsct,tchd->schd', weights.astype(jnp.float32), value_heads)
    return attended.astype(jnp.bfloat16).reshape(query_count, columns, HD)

def reference(tokens, gap_mask, window_reach, row_qkv, row_out, col_qkv, col_out):
    species, columns, features = tokens.shape
    block_count = columns // BLOCK
    normed = lax.map(lambda rows: rms_rows(rows.astype(jnp.float32)).astype(jnp.bfloat16), tokens)
    packed = lax.map(lambda rows: jnp.dot(rows, row_qkv, preferred_element_type=jnp.float32).astype(jnp.bfloat16), normed)
    offsets = jnp.arange(3 * BLOCK, dtype=jnp.int32)

    def segment(array, index):
        return lax.dynamic_slice_in_dim(array, (index * BLOCK).astype(jnp.int32), BLOCK, 1)

    def one_block(block_id):
        before_blk = (block_id + block_count - 1) % block_count
        after_blk = (block_id + 1) % block_count
        own_block = segment(packed, block_id)
        keyval = jnp.concatenate([segment(packed, before_blk)[..., HD:], own_block[..., HD:], segment(packed, after_blk)[..., HD:]], axis=1)
        reach_now = window_reach[block_id]
        before_ok = gap_mask[:, before_blk] == 1
        after_ok = gap_mask[:, after_blk] == 1
        in_before = (offsets < BLOCK) & (offsets >= BLOCK - reach_now)
        in_middle = (offsets >= BLOCK) & (offsets < 2 * BLOCK)
        in_after = (offsets >= 2 * BLOCK) & (offsets < 2 * BLOCK + reach_now)
        usable = in_middle[None, :] | in_before[None, :] & before_ok[:, None] | in_after[None, :] & after_ok[:, None]
        attended = lax.map(lambda item: row_attend(item[0], item[1], item[2]), (own_block[..., :HD], keyval, usable))
        token_block = segment(tokens, block_id)
        middle = token_block.astype(jnp.float32) + jnp.dot(attended.reshape(-1, HD), row_out, preferred_element_type=jnp.float32).reshape(species, BLOCK, features)
        col_normed = rms_rows(middle).astype(jnp.bfloat16)
        col_packed = jnp.dot(col_normed.reshape(-1, features), col_qkv, preferred_element_type=jnp.float32).astype(jnp.bfloat16).reshape(species, BLOCK, 3 * HD)
        alive = gap_mask[:, block_id] == 1
        col_attended = column_attend(col_packed[..., :HD], col_packed[..., HD:], alive)
        result = middle + jnp.dot(col_attended.reshape(-1, HD), col_out, preferred_element_type=jnp.float32).reshape(species, BLOCK, features)
        return result.astype(jnp.bfloat16)
    blocks = lax.map(one_block, jnp.arange(block_count, dtype=jnp.int32))
    return jnp.transpose(blocks, (1, 0, 2, 3)).reshape(species, columns, features)
```

```python
import math

import jax
import jax.numpy as jnp
from jax import lax
from jax.experimental import pallas as pl
from jax.experimental.pallas import tpu as pltpu
from jax.sharding import PartitionSpec as P

HEAD = 64
PAIR = 2 * HEAD
SCALE = HEAD ** (-0.5) / math.log(2.0)
BF = jnp.bfloat16
F32 = jnp.float32
VMEM = pl.BlockSpec(memory_space=pltpu.VMEM)
SMEM = pl.BlockSpec(memory_space=pltpu.SMEM)


def dot(a, b):
    return jnp.dot(a, b, preferred_element_type=F32)


def dot_t(a, b):
    return lax.dot_general(a, b, (((1,), (1,)), ((), ())), preferred_element_type=F32)


def rms(values):
    return values * lax.rsqrt(jnp.mean(values * values, axis=-1, keepdims=True) + 1e-06)


def lower_half(rows):
    return lax.broadcasted_iota(jnp.int32, (rows, PAIR), 1) < HEAD


def one_head(pair, head):
    low = lower_half(pair.shape[0])
    keep = low if head == 0 else ~low
    return jnp.where(keep, pair, jnp.zeros_like(pair))


def values_and_ones(pair, head):
    return jnp.concatenate([one_head(pair, head), one_head(jnp.ones_like(pair), head)], axis=1)


def spread(first, second, rows):
    return jnp.where(
        lower_half(rows),
        jnp.broadcast_to(first, (rows, PAIR)),
        jnp.broadcast_to(second, (rows, PAIR)),
    )


def keyval_kernel(x_ref, w_ref, n_ref, kv0_ref, kv1_ref):
    step = pl.program_id(0)

    @pl.when(step == 0)
    def _():
        n_ref[...] = rms(x_ref[...].astype(F32)).astype(BF)

    out = dot(n_ref[...], w_ref[...]).astype(BF)
    for half in range(2):
        part = out[:, half * PAIR : (half + 1) * PAIR]

        @pl.when(step < 2)
        def _():
            kv0_ref[half] = part

        @pl.when(step >= 2)
        def _():
            kv1_ref[half] = part


def keyval(x, weights):
    rows, features = x.shape
    hd = weights.shape[1] // 3
    grp = hd // 2
    pairs = grp // PAIR
    out = jax.ShapeDtypeStruct((2 * pairs, rows, PAIR), BF)
    return pl.pallas_call(
        keyval_kernel,
        grid=(4,),
        in_specs=[
            pl.BlockSpec((rows, features), lambda j: (0, 0)),
            pl.BlockSpec((features, grp), lambda j: (0, 2 + (j % 2) * 2 + j // 2)),
        ],
        out_specs=[
            pl.BlockSpec((rows, features), lambda j: (0, 0)),
            pl.BlockSpec((pairs, rows, PAIR), lambda j: (jnp.minimum(j, 1), 0, 0)),
            pl.BlockSpec((pairs, rows, PAIR), lambda j: (jnp.maximum(j - 2, 0), 0, 0)),
        ],
        out_shape=[jax.ShapeDtypeStruct((rows, features), BF), out, out],
        compiler_params=pltpu.CompilerParams(vmem_limit_bytes=20 * 2**20),
        name="keyval",
    )(x, weights)


def query_kernel(n_ref, w_ref, q_ref):
    for grp in range(2):
        cols = pl.ds(grp * 2 * PAIR, 2 * PAIR)
        out = (dot(n_ref[...], w_ref[:, cols]) * SCALE).astype(BF)
        q_ref[2 * grp] = out[:, :PAIR]
        q_ref[2 * grp + 1] = out[:, PAIR:]


def queries(normed, weights):
    rows, features = normed.shape
    hd = weights.shape[1] // 3
    return pl.pallas_call(
        query_kernel,
        grid=(1,),
        in_specs=[
            pl.BlockSpec((rows, features), lambda j: (0, 0)),
            pl.BlockSpec((features, hd), lambda j: (0, 0)),
        ],
        out_specs=pl.BlockSpec((hd // PAIR, rows, PAIR), lambda j: (0, 0, 0)),
        out_shape=jax.ShapeDtypeStruct((hd // PAIR, rows, PAIR), BF),
        compiler_params=pltpu.CompilerParams(vmem_limit_bytes=20 * 2**20),
        name="queries",
    )(normed, weights)


def window_of(gap_ref, reach_ref, blocklen, blocks, fast):
    block = lax.axis_index("ctx")
    species = lax.axis_index("species")
    odd = lax.rem(block, 2)
    before = odd == 1 if fast else odd == 0
    other = jnp.where(before, lax.rem(block + blocks - 1, blocks), lax.rem(block + 1, blocks))
    reach = reach_ref[block]
    low = jnp.where(before, blocklen - reach, 0)
    high = jnp.where(before, blocklen, reach)
    high = jnp.where(gap_ref[species, other] == 1, high, 0)
    cols = lax.broadcasted_iota(jnp.int32, (1, blocklen), 1)
    return (cols >= low) & (cols < high)


ROWS = 256


def near_kernel(blocks, gap_ref, reach_ref, q_ref, o0, o1, f0, f1, acc_ref, max_ref):
    rows = q_ref.shape[1]
    seen = window_of(gap_ref, reach_ref, rows, blocks, True)
    for grp, (own, fast) in enumerate(((o0, f0), (o1, f1))):

        def pair_step(i, carry):
            p = 2 * grp + i
            keys_own, keys_fast = own[i], fast[i]
            vals = (own[2 + i], fast[2 + i])
            va = jnp.concatenate([values_and_ones(v, h) for h in range(2) for v in vals], axis=0)
            for t in range(rows // ROWS):
                part = pl.ds(t * ROWS, ROWS)
                q = q_ref[p, part]
                tops, probs = [], []
                for h in range(2):
                    qh = one_head(q, h)
                    so = dot_t(qh, keys_own)
                    sf = jnp.where(seen, dot_t(qh, keys_fast), -1e30)
                    top = jnp.maximum(
                        jnp.max(so, axis=-1, keepdims=True), jnp.max(sf, axis=-1, keepdims=True)
                    )
                    tops.append(top)
                    probs += [jnp.exp2(so - top).astype(BF), jnp.exp2(sf - top).astype(BF)]
                acc_ref[p, part] = dot(jnp.concatenate(probs, axis=1), va)
                max_ref[p, part] = spread(tops[0], tops[1], ROWS)
            return carry

        lax.fori_loop(0, 2, pair_step, 0)


def near_attend(gap_mask, reach, q, own, fast):
    pairs, rows, _ = q.shape
    blocks = gap_mask.shape[1]

    def kernel(*refs):
        near_kernel(blocks, *refs)

    return pl.pallas_call(
        kernel,
        in_specs=[SMEM, SMEM] + [VMEM] * 5,
        out_specs=[VMEM, VMEM],
        out_shape=[
            jax.ShapeDtypeStruct((pairs, rows, 2 * PAIR), F32),
            jax.ShapeDtypeStruct((pairs, rows, PAIR), F32),
        ],
        compiler_params=pltpu.CompilerParams(vmem_limit_bytes=24 * 2**20),
        name="near_attend",
    )(gap_mask, reach, q, *own, *fast)


def far_kernel(grp, blocks, gap_ref, reach_ref, q_ref, kv_ref, acc_ref, max_ref, out_ref):
    rows = q_ref.shape[1]
    seen = window_of(gap_ref, reach_ref, rows, blocks, False)
    for i in range(2):
        p = 2 * grp + i
        keys, v = kv_ref[i], kv_ref[2 + i]
        va = jnp.concatenate([values_and_ones(v, h) for h in range(2)], axis=0)
        for t in range(rows // ROWS):
            part = pl.ds(t * ROWS, ROWS)
            q = q_ref[p, part]
            old = max_ref[p, part]
            scales, probs = [], []
            for h in range(2):
                s = jnp.where(seen, dot_t(one_head(q, h), keys), -1e30)
                before = old[:, h * HEAD : h * HEAD + 1]
                top = jnp.maximum(jnp.max(s, axis=-1, keepdims=True), before)
                scales.append(jnp.exp2(before - top))
                probs.append(jnp.exp2(s - top).astype(BF))
            acc = dot(jnp.concatenate(probs, axis=1), va)
            scale = spread(scales[0], scales[1], ROWS)
            old_acc = acc_ref[p, part]
            num = acc[:, :PAIR] + old_acc[:, :PAIR] * scale
            den = acc[:, PAIR:] + old_acc[:, PAIR:] * scale
            out_ref[part, i * PAIR : (i + 1) * PAIR] = (num / den).astype(BF)


def far_attend(grp, gap_mask, reach, q, kv, acc, top):
    pairs, rows, _ = q.shape
    blocks = gap_mask.shape[1]

    def kernel(*refs):
        far_kernel(grp, blocks, *refs)

    return pl.pallas_call(
        kernel,
        in_specs=[SMEM, SMEM] + [VMEM] * 4,
        out_specs=VMEM,
        out_shape=jax.ShapeDtypeStruct((rows, pairs // 2 * PAIR), BF),
        compiler_params=pltpu.CompilerParams(vmem_limit_bytes=24 * 2**20),
        name=f"far_attend{grp}",
    )(gap_mask, reach, q, kv, acc, top)


def middle_kernel(x_ref, a0_ref, a1_ref, w_ref, mid_ref, send_ref):
    half = a0_ref.shape[1]
    mid = x_ref[...].astype(F32) + dot(a0_ref[...], w_ref[:half]) + dot(a1_ref[...], w_ref[half:])
    mid_ref[...] = mid
    send_ref[...] = mid.astype(BF)


def middle_of(x, att0, att1, weights):
    rows, features = x.shape
    return pl.pallas_call(
        middle_kernel,
        in_specs=[VMEM] * 4,
        out_specs=[VMEM, VMEM],
        out_shape=[
            jax.ShapeDtypeStruct((rows, features), F32),
            jax.ShapeDtypeStruct((rows, features), BF),
        ],
        compiler_params=pltpu.CompilerParams(vmem_limit_bytes=16 * 2**20),
        name="middle",
    )(x, att0, att1, weights)


COLS = 16


def column_kernel(gap_ref, mid_ref, w_ref, out_ref, pack_ref):
    species, columns, features = mid_ref.shape
    hd = out_ref.shape[2]
    pairs = hd // PAIR
    n = rms(mid_ref[...].reshape(species * columns, features).astype(F32)).astype(BF)
    for j in range(3 * pairs // 2):
        out = dot(n, w_ref[:, 2 * j * PAIR : 2 * (j + 1) * PAIR])
        if j < pairs // 2:
            out = out * SCALE
        out = out.astype(BF).reshape(species, columns, 2 * PAIR)
        pack_ref[2 * j] = out[:, :, :PAIR]
        pack_ref[2 * j + 1] = out[:, :, PAIR:]
    block = lax.axis_index("ctx")
    rows = species * COLS
    qrow = lax.broadcasted_iota(jnp.int32, (rows, rows), 0)
    krow = lax.broadcasted_iota(jnp.int32, (rows, rows), 1)
    alive = jnp.zeros((rows, rows), jnp.int32)
    for t in range(species):
        alive = jnp.where(lax.div(krow, COLS) == t, gap_ref[t, block], alive)
    seen = (lax.rem(qrow, COLS) == lax.rem(krow, COLS)) & (alive == 1)
    seen = jnp.concatenate([seen, seen], axis=0)
    for j in range(columns // COLS):
        part = pl.ds(j * COLS, COLS)
        for p in range(pairs):
            q = pack_ref[p, :, part, :].reshape(rows, PAIR)
            k = pack_ref[pairs + p, :, part, :].reshape(rows, PAIR)
            v = pack_ref[2 * pairs + p, :, part, :].reshape(rows, PAIR)
            qs = jnp.concatenate([one_head(q, 0), one_head(q, 1)], axis=0)
            s = jnp.where(seen, dot_t(qs, k), -1e30)
            prob = jnp.exp2(s - jnp.max(s, axis=-1, keepdims=True)).astype(BF)
            prob = jnp.concatenate([prob[:rows], prob[rows:]], axis=1)
            va = jnp.concatenate([values_and_ones(v, 0), values_and_ones(v, 1)], axis=0)
            acc = dot(prob, va)
            att = (acc[:, :PAIR] / acc[:, PAIR:]).astype(BF)
            out_ref[:, part, p * PAIR : (p + 1) * PAIR] = att.reshape(species, COLS, PAIR)


def column_attend(gap_mask, mid, weights):
    species, columns, _ = mid.shape
    hd = weights.shape[1] // 3
    return pl.pallas_call(
        column_kernel,
        in_specs=[SMEM, VMEM, VMEM],
        out_specs=VMEM,
        out_shape=jax.ShapeDtypeStruct((species, columns, hd), BF),
        scratch_shapes=[pltpu.VMEM((3 * hd // PAIR, species, columns, PAIR), BF)],
        compiler_params=pltpu.CompilerParams(vmem_limit_bytes=24 * 2**20),
        name="column_attend",
    )(gap_mask, mid, weights)


def last_kernel(mid_ref, att_ref, w_ref, out_ref):
    out_ref[...] = (mid_ref[...] + dot(att_ref[...], w_ref[...])).astype(BF)


def last(mid, att, weights):
    rows, features = mid.shape
    hd = att.shape[1]
    tile = rows // 4
    return pl.pallas_call(
        last_kernel,
        grid=(rows // tile,),
        in_specs=[
            pl.BlockSpec((tile, features), lambda i: (i, 0)),
            pl.BlockSpec((tile, hd), lambda i: (i, 0)),
            pl.BlockSpec((hd, features), lambda i: (0, 0)),
        ],
        out_specs=pl.BlockSpec((tile, features), lambda i: (i, 0)),
        out_shape=jax.ShapeDtypeStruct((rows, features), BF),
        compiler_params=pltpu.CompilerParams(vmem_limit_bytes=16 * 2**20),
        name="last",
    )(mid, att, weights)


def body(tokens, gap_mask, window_reach, row_qkv, row_out, col_qkv, col_out):
    _, blocklen, features = tokens.shape
    hd = row_out.shape[0]
    blocks = lax.axis_size("ctx")
    species = lax.axis_size("species")
    near = [(i, i ^ 1) for i in range(blocks)]
    far = [(i, (i + 1 if i % 2 else i - 1) % blocks) for i in range(blocks)]
    x = tokens.reshape(blocklen, features)

    normed, kv0, kv1 = keyval(x, row_qkv)
    far0 = lax.ppermute(kv0, "ctx", far)
    fast0 = lax.ppermute(kv0, "ctx", near)
    fast1 = lax.ppermute(kv1, "ctx", near)
    far1 = lax.ppermute(kv1, "ctx", far)
    q = queries(normed, row_qkv)
    acc, top = near_attend(gap_mask, window_reach, q, (kv0, kv1), (fast0, fast1))
    att0 = far_attend(0, gap_mask, window_reach, q, far0, acc, top)
    att1 = far_attend(1, gap_mask, window_reach, q, far1, acc, top)
    mid, send = middle_of(x, att0, att1, row_out)

    columns = blocklen // species
    got = lax.all_to_all(send.reshape(species, columns, features), "species", 0, 0)
    col_att = column_attend(gap_mask, got, col_qkv)
    back = lax.all_to_all(col_att, "species", 0, 0)
    out = last(mid, back.reshape(blocklen, hd), col_out)
    return out.reshape(1, blocklen, features)


def solution(mesh):
    placed = (P("species", "ctx", None), P(), P(), P(), P(), P(), P())
    return jax.shard_map(
        body, mesh=mesh, in_specs=placed, out_specs=P("species", "ctx", None), check_vma=False
    )
```

```python
import math

import jax
import jax.numpy as jnp
from jax import lax
from jax.experimental import pallas as pl
from jax.experimental.pallas import tpu as pltpu
from jax.sharding import PartitionSpec as P

HEAD = 64
PAIR = 2 * HEAD
ROWS = 128
COLS = 16
FAR = ((0, 1, 2), (3,))
SCALE = HEAD ** (-0.5) / math.log(2.0)
BF = jnp.bfloat16
F32 = jnp.float32
VMEM = pl.BlockSpec(memory_space=pltpu.VMEM)
SMEM = pl.BlockSpec(memory_space=pltpu.SMEM)
HBM = pl.BlockSpec(memory_space=pltpu.HBM)


def dot(a, b):
    return jnp.dot(a, b, preferred_element_type=F32)


def dot_t(a, b):
    return lax.dot_general(a, b, (((1,), (1,)), ((), ())), preferred_element_type=F32)


def rms(values):
    return values * lax.rsqrt(jnp.mean(values * values, axis=-1, keepdims=True) + 1e-06)


def lower_half(rows):
    return lax.broadcasted_iota(jnp.int32, (rows, PAIR), 1) < HEAD


def one_head(pair, head):
    low = lower_half(pair.shape[0])
    keep = low if head == 0 else ~low
    return jnp.where(keep, pair, jnp.zeros_like(pair))


def values_and_ones(pair, head):
    return jnp.concatenate([one_head(pair, head), one_head(jnp.ones_like(pair), head)], axis=1)


def cost(flops, bytes_accessed):
    return pl.CostEstimate(flops=flops, bytes_accessed=bytes_accessed, transcendentals=0)


def window_of(gap_ref, reach_ref, blocklen, blocks, fast):
    block = lax.axis_index("ctx")
    species = lax.axis_index("species")
    odd = lax.rem(block, 2)
    before = odd == 1 if fast else odd == 0
    other = jnp.where(before, lax.rem(block + blocks - 1, blocks), lax.rem(block + 1, blocks))
    reach = reach_ref[block]
    low = jnp.where(before, blocklen - reach, 0)
    high = jnp.where(before, blocklen, reach)
    high = jnp.where(gap_ref[species, other] == 1, high, 0)
    cols = lax.broadcasted_iota(jnp.int32, (8, blocklen), 1)
    return jnp.where((cols >= low) & (cols < high), 1.0, 0.0)


def keyval_kernel(x_hbm, w_hbm, x_ref, n_ref, wq_ref, kv_ref, *refs):
    far_refs = refs[: len(FAR)]
    w_ref, xsem, wsem, qsem = refs[len(FAR) :]
    rows = x_ref.shape[0]
    hd = wq_ref.shape[1]
    pairs = hd // PAIR
    parts = xsem.shape[0]
    tile = rows // parts
    xs = [
        pltpu.make_async_copy(
            x_hbm.at[pl.ds(i * tile, tile)], x_ref.at[pl.ds(i * tile, tile)], xsem.at[i]
        )
        for i in range(parts)
    ]
    ws = [
        pltpu.make_async_copy(
            w_hbm.at[:, pl.ds(hd + i * hd // 2, hd // 2)],
            w_ref.at[:, pl.ds(i * hd // 2, hd // 2)],
            wsem.at[i],
        )
        for i in range(4)
    ]
    wq = pltpu.make_async_copy(w_hbm.at[:, pl.ds(0, hd)], wq_ref, qsem)
    for copy in xs + ws:
        copy.start()
    wq.start()
    for i in range(parts):
        xs[i].wait()
        part = pl.ds(i * tile, tile)
        n_ref[part] = rms(x_ref[part].astype(F32)).astype(BF)
    for copy in ws:
        copy.wait()
    out = dot(n_ref[...], w_ref[...]).astype(BF)
    for p in range(2 * pairs):
        kv_ref[p] = out[:, p * PAIR : (p + 1) * PAIR]
    for far_ref, group in zip(far_refs, FAR):
        for i, p in enumerate(group):
            far_ref[i] = out[:, p * PAIR : (p + 1) * PAIR]
            far_ref[len(group) + i] = out[:, hd + p * PAIR : hd + (p + 1) * PAIR]
    wq.wait()


def keyval(x, weights):
    rows, features = x.shape
    hd = weights.shape[1] // 3
    pairs = hd // PAIR
    out = pl.pallas_call(
        keyval_kernel,
        in_specs=[HBM] * 2,
        out_specs=[VMEM] * (4 + len(FAR)),
        out_shape=[
            jax.ShapeDtypeStruct((rows, features), BF),
            jax.ShapeDtypeStruct((rows, features), BF),
            jax.ShapeDtypeStruct((features, hd), BF),
            jax.ShapeDtypeStruct((2 * pairs, rows, PAIR), BF),
            *[jax.ShapeDtypeStruct((2 * len(group), rows, PAIR), BF) for group in FAR],
        ],
        scratch_shapes=[
            pltpu.VMEM((features, 2 * hd), BF),
            pltpu.SemaphoreType.DMA((4,)),
            pltpu.SemaphoreType.DMA((4,)),
            pltpu.SemaphoreType.DMA,
        ],
        compiler_params=pltpu.CompilerParams(vmem_limit_bytes=48 * 2**20),
        cost_estimate=cost(2 * rows * features * 2 * hd, 6 * 2**20),
        name="keyval",
    )(x, weights)
    return *out[:4], out[4:]


def query_kernel(gap_ref, reach_ref, n_ref, w_ref, q_ref, mask_ref, alive_ref):
    out = (dot(n_ref[...], w_ref[...]) * SCALE).astype(BF)
    for p in range(q_ref.shape[0]):
        q_ref[p] = out[:, p * PAIR : (p + 1) * PAIR]
    species, blocks = gap_ref.shape
    for i in range(2):
        mask_ref[i] = window_of(gap_ref, reach_ref, n_ref.shape[0], blocks, i == 0)
    lanes = lax.broadcasted_iota(jnp.int32, alive_ref.shape, 1)
    alive = jnp.zeros(alive_ref.shape, jnp.int32)
    for t in range(species):
        alive = jnp.where(lax.div(lanes, COLS) == t, gap_ref[t, lax.axis_index("ctx")], alive)
    alive_ref[...] = alive


def queries(gap_mask, reach, normed, weights):
    rows, features = normed.shape
    hd = weights.shape[1]
    species = gap_mask.shape[0]
    return pl.pallas_call(
        query_kernel,
        in_specs=[SMEM, SMEM, VMEM, VMEM],
        out_specs=[VMEM] * 3,
        out_shape=[
            jax.ShapeDtypeStruct((hd // PAIR, rows, PAIR), BF),
            jax.ShapeDtypeStruct((2, 8, rows), F32),
            jax.ShapeDtypeStruct((8, species * COLS), jnp.int32),
        ],
        compiler_params=pltpu.CompilerParams(vmem_limit_bytes=16 * 2**20),
        cost_estimate=cost(2 * rows * features * hd, 2**20),
        name="queries",
    )(gap_mask, reach, normed, weights)


def near_kernel(mask_ref, q_ref, own, fast, acc_ref, max_ref):
    pairs, rows, _ = q_ref.shape
    seen = mask_ref[0, :1] > 0.5

    def scores(p, t):
        q = q_ref[p, pl.ds(t * ROWS, ROWS)]
        heads = [one_head(q, h) for h in range(2)]
        return [(dot_t(q, own[p]), dot_t(q, fast[p])) for q in heads]

    def finish(p, t, found, va):
        part = pl.ds(t * ROWS, ROWS)
        probs = []
        for h, (so, sf) in enumerate(found):
            sf = jnp.where(seen, sf, -1e30)
            top = jnp.maximum(
                jnp.max(so, axis=-1, keepdims=True), jnp.max(sf, axis=-1, keepdims=True)
            )
            max_ref[2 * p + h, part] = jnp.broadcast_to(top, (ROWS, PAIR))
            probs += [jnp.exp2(so - top).astype(BF), jnp.exp2(sf - top).astype(BF)]
        acc_ref[p, part] = dot(jnp.concatenate(probs, axis=1), va)

    late = None
    for p in range(pairs):
        vals = (own[pairs + p], fast[pairs + p])
        va = jnp.concatenate([values_and_ones(v, h) for h in range(2) for v in vals], axis=0)
        for t in range(rows // ROWS):
            found = scores(p, t)
            if late is not None:
                finish(*late)
            late = (p, t, found, va)
    finish(*late)


def near_attend(mask, q, own, fast):
    pairs, rows, _ = q.shape
    return pl.pallas_call(
        near_kernel,
        in_specs=[VMEM] * 4,
        out_specs=[VMEM, VMEM],
        out_shape=[
            jax.ShapeDtypeStruct((pairs, rows, 2 * PAIR), F32),
            jax.ShapeDtypeStruct((2 * pairs, rows, PAIR), F32),
        ],
        compiler_params=pltpu.CompilerParams(vmem_limit_bytes=24 * 2**20),
        cost_estimate=cost(32 * rows * rows * PAIR * pairs, 2**23),
        name="near_attend",
    )(mask, q, own, fast)


def far_kernel(group, mask_ref, q_ref, kv_ref, acc_ref, max_ref, *refs):
    out_ref = refs[-1]
    rows = q_ref.shape[1]
    seen = mask_ref[1, :1] > 0.5

    def scores(i, t):
        q = q_ref[group[i], pl.ds(t * ROWS, ROWS)]
        return [dot_t(one_head(q, h), kv_ref[i]) for h in range(2)]

    def finish(i, t, found, va):
        p = group[i]
        part = pl.ds(t * ROWS, ROWS)
        scales, probs = [], []
        for h, s in enumerate(found):
            s = jnp.where(seen, s, -1e30)
            before = max_ref[2 * p + h, part]
            top = jnp.maximum(jnp.max(s, axis=-1, keepdims=True), before)
            scales.append(jnp.exp2(before - top))
            probs.append(jnp.exp2(s - jnp.concatenate([top] * (rows // PAIR), axis=1)).astype(BF))
        acc = dot(jnp.concatenate(probs, axis=1), va)
        scale = jnp.where(lower_half(ROWS), scales[0], scales[1])
        old = acc_ref[p, part]
        num = acc[:, :PAIR] + old[:, :PAIR] * scale
        den = acc[:, PAIR:] + old[:, PAIR:] * scale
        out_ref[part, p * PAIR : (p + 1) * PAIR] = (num / den).astype(BF)

    late = None
    for i in range(len(group)):
        vals = kv_ref[len(group) + i]
        va = jnp.concatenate([values_and_ones(vals, h) for h in range(2)], axis=0)
        for t in range(rows // ROWS):
            found = scores(i, t)
            if late is not None:
                finish(*late)
            late = (i, t, found, va)
    finish(*late)


def far_attend(group, mask, q, kv, acc, top, att):
    pairs, rows, _ = q.shape

    def kernel(*refs):
        far_kernel(group, *refs)

    return pl.pallas_call(
        kernel,
        in_specs=[VMEM] * (5 + len(att)),
        out_specs=VMEM,
        out_shape=jax.ShapeDtypeStruct((rows, pairs * PAIR), BF),
        input_output_aliases={5: 0} if att else {},
        compiler_params=pltpu.CompilerParams(vmem_limit_bytes=24 * 2**20),
        cost_estimate=cost(16 * rows * rows * PAIR * len(group), 2**21),
        name=f"far_attend{group[0]}",
    )(mask, q, kv, acc, top, *att)


def middle_kernel(x_ref, att_ref, w_ref, mid_ref, send_ref):
    mid = x_ref[...].astype(F32) + dot(att_ref[...], w_ref[...])
    mid_ref[...] = mid
    send_ref[...] = mid.astype(BF)


def middle_of(x, att, weights):
    rows, features = x.shape
    return pl.pallas_call(
        middle_kernel,
        in_specs=[VMEM] * 3,
        out_specs=[VMEM, VMEM],
        out_shape=[
            jax.ShapeDtypeStruct((rows, features), F32),
            jax.ShapeDtypeStruct((rows, features), BF),
        ],
        compiler_params=pltpu.CompilerParams(vmem_limit_bytes=16 * 2**20),
        cost_estimate=cost(2 * rows * features * weights.shape[0], 2**22),
        name="middle",
    )(x, att, weights)


def column_kernel(alive_ref, mid_ref, w_ref, out_ref, pack_ref):
    species, columns, features = mid_ref.shape
    hd = out_ref.shape[2]
    pairs = hd // PAIR
    n = rms(mid_ref[...].reshape(species * columns, features).astype(F32)).astype(BF)
    for j in range(3):
        out = dot(n, w_ref[:, j * hd : (j + 1) * hd])
        if j == 0:
            out = out * SCALE
        out = out.astype(BF).reshape(species, columns, hd)
        for p in range(pairs):
            pack_ref[j * pairs + p] = out[:, :, p * PAIR : (p + 1) * PAIR]
    rows = species * COLS
    qrow = lax.broadcasted_iota(jnp.int32, (rows, rows), 0)
    krow = lax.broadcasted_iota(jnp.int32, (rows, rows), 1)
    seen = (lax.rem(qrow, COLS) == lax.rem(krow, COLS)) & (alive_ref[:1] == 1)
    seen = jnp.concatenate([seen, seen], axis=0)
    for j in range(columns // COLS):
        part = pl.ds(j * COLS, COLS)
        for p in range(pairs):
            q = pack_ref[p, :, part, :].reshape(rows, PAIR)
            k = pack_ref[pairs + p, :, part, :].reshape(rows, PAIR)
            v = pack_ref[2 * pairs + p, :, part, :].reshape(rows, PAIR)
            qs = jnp.concatenate([one_head(q, 0), one_head(q, 1)], axis=0)
            s = jnp.where(seen, dot_t(qs, k), -1e30)
            prob = jnp.exp2(s - jnp.max(s, axis=-1, keepdims=True)).astype(BF)
            prob = jnp.concatenate([prob[:rows], prob[rows:]], axis=1)
            va = jnp.concatenate([values_and_ones(v, 0), values_and_ones(v, 1)], axis=0)
            acc = dot(prob, va)
            att = (acc[:, :PAIR] / acc[:, PAIR:]).astype(BF)
            out_ref[:, part, p * PAIR : (p + 1) * PAIR] = att.reshape(species, COLS, PAIR)


def column_attend(alive, mid, weights):
    species, columns, _ = mid.shape
    hd = weights.shape[1] // 3
    return pl.pallas_call(
        column_kernel,
        in_specs=[VMEM] * 3,
        out_specs=VMEM,
        out_shape=jax.ShapeDtypeStruct((species, columns, hd), BF),
        scratch_shapes=[pltpu.VMEM((3 * hd // PAIR, species, columns, PAIR), BF)],
        compiler_params=pltpu.CompilerParams(vmem_limit_bytes=24 * 2**20),
        name="column_attend",
    )(alive, mid, weights)


def last_kernel(mid_ref, att_ref, w_ref, out_ref):
    tile = out_ref.shape[0]
    part = pl.ds(pl.multiple_of(pl.program_id(0) * tile, tile), tile)
    out_ref[...] = (mid_ref[part] + dot(att_ref[part], w_ref[...])).astype(BF)


def last(mid, att, weights):
    rows, features = mid.shape
    tile = rows // 2
    return pl.pallas_call(
        last_kernel,
        grid=(rows // tile,),
        in_specs=[VMEM] * 3,
        out_specs=pl.BlockSpec((tile, features), lambda i: (i, 0)),
        out_shape=jax.ShapeDtypeStruct((rows, features), BF),
        compiler_params=pltpu.CompilerParams(vmem_limit_bytes=16 * 2**20),
        name="last",
    )(mid, att, weights)


def body(tokens, gap_mask, window_reach, row_qkv, row_out, col_qkv, col_out):
    _, blocklen, features = tokens.shape
    hd = row_out.shape[0]
    blocks = lax.axis_size("ctx")
    species = lax.axis_size("species")
    columns = blocklen // species
    near = [(i, i ^ 1) for i in range(blocks)]
    far = [(i, (i + 1 if i % 2 else i - 1) % blocks) for i in range(blocks)]
    x = tokens.reshape(blocklen, features)

    def by_column(array):
        return lax.all_to_all(array.reshape(species, columns, array.shape[1]), "species", 0, 0)

    x, normed, wq, own, sends = keyval(x, row_qkv)
    q, mask, alive = queries(gap_mask, window_reach, normed, wq)
    q, last_send = lax.optimization_barrier((q, sends[-1]))
    fars = [lax.ppermute(kv, "ctx", far) for kv in (*sends[:-1], last_send)]
    fast = lax.ppermute(own, "ctx", near)
    acc, top = near_attend(mask, q, own, fast)
    att = []
    for group, kv in zip(FAR, fars):
        att = [far_attend(group, mask, q, kv, acc, top, att)]
    mid, send = middle_of(x, att[0], row_out)
    col_att = column_attend(alive, by_column(send), col_qkv)
    back = lax.all_to_all(col_att, "species", 0, 0)
    out = last(mid, back.reshape(blocklen, hd), col_out)
    return out.reshape(1, blocklen, features)


def solution(mesh):
    placed = (P("species", "ctx", None), P(), P(), P(), P(), P(), P())
    return jax.shard_map(
        body, mesh=mesh, in_specs=placed, out_specs=P("species", "ctx", None), check_vma=False
    )
```

```python
import math

import jax
import jax.numpy as jnp
from jax import lax
from jax.experimental import pallas as pl
from jax.experimental.pallas import tpu as pltpu
from jax.sharding import PartitionSpec as P

HEAD = 64
PAIR = 2 * HEAD
ROWS = 128
COLS = 16
NEAR = ((0, 1), (2, 3))
SCALE = HEAD ** (-0.5) / math.log(2.0)
BF = jnp.bfloat16
F32 = jnp.float32
VMEM = pl.BlockSpec(memory_space=pltpu.VMEM)
SMEM = pl.BlockSpec(memory_space=pltpu.SMEM)
HBM = pl.BlockSpec(memory_space=pltpu.HBM)


def dot(a, b):
    return jnp.dot(a, b, preferred_element_type=F32)


def dot_t(a, b):
    return lax.dot_general(a, b, (((1,), (1,)), ((), ())), preferred_element_type=F32)


def rms(values):
    return values * lax.rsqrt(jnp.mean(values * values, axis=-1, keepdims=True) + 1e-06)


def lower_half(rows):
    return lax.broadcasted_iota(jnp.int32, (rows, PAIR), 1) < HEAD


def one_head(pair, head):
    low = lower_half(pair.shape[0])
    keep = low if head == 0 else ~low
    return jnp.where(keep, pair, jnp.zeros_like(pair))


def values_and_ones(pair, head):
    return jnp.concatenate([one_head(pair, head), one_head(jnp.ones_like(pair), head)], axis=1)


def cost(flops, bytes_accessed):
    return pl.CostEstimate(flops=flops, bytes_accessed=bytes_accessed, transcendentals=0)


def window_of(gap_ref, reach_ref, blocklen, blocks, fast):
    block = lax.axis_index("ctx")
    species = lax.axis_index("species")
    odd = lax.rem(block, 2)
    before = odd == 1 if fast else odd == 0
    other = jnp.where(before, lax.rem(block + blocks - 1, blocks), lax.rem(block + 1, blocks))
    reach = reach_ref[block]
    low = jnp.where(before, blocklen - reach, 0)
    high = jnp.where(before, blocklen, reach)
    high = jnp.where(gap_ref[species, other] == 1, high, 0)
    cols = lax.broadcasted_iota(jnp.int32, (8, blocklen), 1)
    return jnp.where((cols >= low) & (cols < high), 1.0, 0.0)


def keyval_kernel(x_hbm, w_hbm, x_ref, n_ref, wq_ref, wk_ref, wv_ref, *refs):
    groups = NEAR
    kv_refs = refs[: len(groups)]
    xsem, wsem, qsem = refs[len(groups) :]
    rows = x_ref.shape[0]
    hd = wq_ref.shape[1]
    parts = xsem.shape[0]
    tile = rows // parts
    xs = [
        pltpu.make_async_copy(
            x_hbm.at[pl.ds(i * tile, tile)], x_ref.at[pl.ds(i * tile, tile)], xsem.at[i]
        )
        for i in range(parts)
    ]
    ws = [
        pltpu.make_async_copy(w_hbm.at[:, pl.ds(i * hd, hd)], w_ref, wsem.at[i - 1])
        for i, w_ref in ((1, wk_ref), (2, wv_ref))
    ]
    wq = pltpu.make_async_copy(w_hbm.at[:, pl.ds(0, hd)], wq_ref, qsem)
    for copy in xs + ws:
        copy.start()
    wq.start()
    for i in range(parts):
        xs[i].wait()
        part = pl.ds(i * tile, tile)
        n_ref[part] = rms(x_ref[part].astype(F32)).astype(BF)
    for copy in ws:
        copy.wait()
    keys = dot(n_ref[...], wk_ref[...]).astype(BF)
    values = dot(n_ref[...], wv_ref[...]).astype(BF)
    for kv_ref, group in zip(kv_refs, groups):
        for i, p in enumerate(group):
            kv_ref[i] = keys[:, p * PAIR : (p + 1) * PAIR]
            kv_ref[len(group) + i] = values[:, p * PAIR : (p + 1) * PAIR]
    wq.wait()


def keyval(x, weights):
    rows, features = x.shape
    hd = weights.shape[1] // 3
    out = pl.pallas_call(
        keyval_kernel,
        in_specs=[HBM] * 2,
        out_specs=[VMEM] * (5 + len(NEAR)),
        out_shape=[
            jax.ShapeDtypeStruct((rows, features), BF),
            jax.ShapeDtypeStruct((rows, features), BF),
            jax.ShapeDtypeStruct((features, hd), BF),
            jax.ShapeDtypeStruct((features, hd), BF),
            jax.ShapeDtypeStruct((features, hd), BF),
            *[jax.ShapeDtypeStruct((2 * len(group), rows, PAIR), BF) for group in NEAR],
        ],
        scratch_shapes=[
            pltpu.SemaphoreType.DMA((4,)),
            pltpu.SemaphoreType.DMA((2,)),
            pltpu.SemaphoreType.DMA,
        ],
        compiler_params=pltpu.CompilerParams(vmem_limit_bytes=47 * 2**20),
        cost_estimate=cost(1, 1),
        name="keyval",
    )(x, weights)
    return *out[:3], out[3:5], out[5:]


def query_kernel(gap_ref, reach_ref, n_ref, w_ref, q_ref, mask_ref, alive_ref):
    out = (dot(n_ref[...], w_ref[...]) * SCALE).astype(BF)
    for p in range(q_ref.shape[0]):
        q_ref[p] = out[:, p * PAIR : (p + 1) * PAIR]
    species, blocks = gap_ref.shape
    for i in range(2):
        mask_ref[i] = window_of(gap_ref, reach_ref, n_ref.shape[0], blocks, i == 0)
    lanes = lax.broadcasted_iota(jnp.int32, alive_ref.shape, 1)
    alive = jnp.zeros(alive_ref.shape, jnp.int32)
    for t in range(species):
        alive = jnp.where(lax.div(lanes, COLS) == t, gap_ref[t, lax.axis_index("ctx")], alive)
    alive_ref[...] = alive


def queries(gap_mask, reach, normed, weights):
    rows, features = normed.shape
    hd = weights.shape[1]
    species = gap_mask.shape[0]
    return pl.pallas_call(
        query_kernel,
        in_specs=[SMEM, SMEM, VMEM, VMEM],
        out_specs=[VMEM] * 3,
        out_shape=[
            jax.ShapeDtypeStruct((hd // PAIR, rows, PAIR), BF),
            jax.ShapeDtypeStruct((2, 8, rows), F32),
            jax.ShapeDtypeStruct((8, species * COLS), jnp.int32),
        ],
        compiler_params=pltpu.CompilerParams(vmem_limit_bytes=16 * 2**20),
        cost_estimate=cost(1, 1),
        name="queries",
    )(gap_mask, reach, normed, weights)


def near_kernel(mask_ref, q_ref, *refs):
    acc_ref, max_ref = refs[-2:]
    owns, fasts = refs[: len(NEAR)], refs[len(NEAR) : -2]
    pairs, rows, _ = q_ref.shape
    seen = mask_ref[0, :1] > 0.5

    def scores(p, t, keys_own, keys_fast):
        q = q_ref[p, pl.ds(t * ROWS, ROWS)]
        heads = [one_head(q, h) for h in range(2)]
        return [(dot_t(q, keys_own), dot_t(q, keys_fast)) for q in heads]

    def finish(p, t, found, va):
        part = pl.ds(t * ROWS, ROWS)
        probs = []
        for h, (so, sf) in enumerate(found):
            sf = jnp.where(seen, sf, -1e30)
            top = jnp.maximum(
                jnp.max(so, axis=-1, keepdims=True), jnp.max(sf, axis=-1, keepdims=True)
            )
            max_ref[2 * p + h, part] = jnp.broadcast_to(top, (ROWS, PAIR))
            probs += [jnp.exp2(so - top).astype(BF), jnp.exp2(sf - top).astype(BF)]
        acc_ref[p, part] = dot(jnp.concatenate(probs, axis=1), va)

    late = None
    for group, own, fast in zip(NEAR, owns, fasts):
        for i, p in enumerate(group):
            vals = (own[len(group) + i], fast[len(group) + i])
            va = jnp.concatenate([values_and_ones(v, h) for h in range(2) for v in vals], axis=0)
            for t in range(rows // ROWS):
                found = scores(p, t, own[i], fast[i])
                if late is not None:
                    finish(*late)
                late = (p, t, found, va)
    finish(*late)


def near_attend(mask, q, own, fast):
    pairs, rows, _ = q.shape
    return pl.pallas_call(
        near_kernel,
        in_specs=[VMEM] * (2 + 2 * len(NEAR)),
        out_specs=[VMEM, VMEM],
        out_shape=[
            jax.ShapeDtypeStruct((pairs, rows, 2 * PAIR), F32),
            jax.ShapeDtypeStruct((2 * pairs, rows, PAIR), F32),
        ],
        compiler_params=pltpu.CompilerParams(vmem_limit_bytes=24 * 2**20),
        cost_estimate=cost(1, 1),
        name="near_attend",
    )(mask, q, *own, *fast)


def far_kernel(mask_ref, q_ref, x_ref, wk_ref, wv_ref, acc_ref, max_ref, own_ref, wo_ref, mid_ref, send_ref, kv_ref, att_ref):
    pairs, rows, _ = q_ref.shape
    seen = mask_ref[1, :1] > 0.5
    squares = jnp.mean(jnp.square(x_ref[...].astype(F32)), axis=-1, keepdims=True)
    factor = lax.rsqrt(squares + 1e-06)
    for i, w_ref in enumerate((wk_ref, wv_ref)):
        out = (dot(x_ref[...], w_ref[...]) * factor).astype(BF)
        for p in range(pairs):
            kv_ref[i * pairs + p] = out[:, p * PAIR : (p + 1) * PAIR]

    def scores(p, t):
        q = q_ref[p, pl.ds(t * ROWS, ROWS)]
        return [dot_t(one_head(q, h), kv_ref[p]) for h in range(2)]

    def finish(p, t, found, va):
        part = pl.ds(t * ROWS, ROWS)
        scales, probs = [], []
        for h, s in enumerate(found):
            s = jnp.where(seen, s, -1e30)
            before = max_ref[2 * p + h, part]
            top = jnp.maximum(jnp.max(s, axis=-1, keepdims=True), before)
            scales.append(jnp.exp2(before - top))
            probs.append(jnp.exp2(s - jnp.concatenate([top] * (rows // PAIR), axis=1)).astype(BF))
        acc = dot(jnp.concatenate(probs, axis=1), va)
        scale = jnp.where(lower_half(ROWS), scales[0], scales[1])
        old = acc_ref[p, part]
        num = acc[:, :PAIR] + old[:, :PAIR] * scale
        den = acc[:, PAIR:] + old[:, PAIR:] * scale
        att_ref[part, p * PAIR : (p + 1) * PAIR] = (num / den).astype(BF)

    late = None
    for p in range(pairs):
        va = jnp.concatenate([values_and_ones(kv_ref[pairs + p], h) for h in range(2)], axis=0)
        for t in range(rows // ROWS):
            found = scores(p, t)
            if late is not None:
                finish(*late)
            late = (p, t, found, va)
    finish(*late)
    mid = own_ref[...].astype(F32) + dot(att_ref[...], wo_ref[...])
    mid_ref[...] = mid
    send_ref[...] = mid.astype(BF)


def far_attend(mask, q, x_far, w_kv, acc, top, x, w_out):
    pairs, rows, _ = q.shape
    features = x.shape[1]
    return pl.pallas_call(
        far_kernel,
        in_specs=[VMEM] * 9,
        out_specs=[VMEM] * 2,
        out_shape=[
            jax.ShapeDtypeStruct((rows, features), F32),
            jax.ShapeDtypeStruct((rows, features), BF),
        ],
        scratch_shapes=[
            pltpu.VMEM((2 * pairs, rows, PAIR), BF),
            pltpu.VMEM((rows, pairs * PAIR), BF),
        ],
        compiler_params=pltpu.CompilerParams(vmem_limit_bytes=24 * 2**20),
        cost_estimate=cost(6 * 10**9, 2**23),
        name="far_attend",
    )(mask, q, x_far, *w_kv, acc, top, x, w_out)


def column_kernel(alive_ref, mid_ref, w_ref, out_ref, pack_ref):
    species, columns, features = mid_ref.shape
    hd = out_ref.shape[2]
    pairs = hd // PAIR
    rows = mid_ref[...].reshape(species * columns, features)
    squares = jnp.mean(jnp.square(rows.astype(F32)), axis=-1, keepdims=True)
    factor = lax.rsqrt(squares + 1e-06)
    for j in range(3):
        out = dot(rows, w_ref[:, j * hd : (j + 1) * hd]) * (factor * SCALE if j == 0 else factor)
        out = out.astype(BF).reshape(species, columns, hd)
        for p in range(pairs):
            pack_ref[j * pairs + p] = out[:, :, p * PAIR : (p + 1) * PAIR]
    rows = species * COLS
    qrow = lax.broadcasted_iota(jnp.int32, (rows, rows), 0)
    krow = lax.broadcasted_iota(jnp.int32, (rows, rows), 1)
    seen = (lax.rem(qrow, COLS) == lax.rem(krow, COLS)) & (alive_ref[:1] == 1)
    seen = jnp.concatenate([seen, seen], axis=0)
    for j in range(columns // COLS):
        part = pl.ds(j * COLS, COLS)
        for p in range(pairs):
            q = pack_ref[p, :, part, :].reshape(rows, PAIR)
            k = pack_ref[pairs + p, :, part, :].reshape(rows, PAIR)
            v = pack_ref[2 * pairs + p, :, part, :].reshape(rows, PAIR)
            qs = jnp.concatenate([one_head(q, 0), one_head(q, 1)], axis=0)
            s = jnp.where(seen, dot_t(qs, k), -1e30)
            prob = jnp.exp2(s - jnp.max(s, axis=-1, keepdims=True)).astype(BF)
            prob = jnp.concatenate([prob[:rows], prob[rows:]], axis=1)
            va = jnp.concatenate([values_and_ones(v, 0), values_and_ones(v, 1)], axis=0)
            acc = dot(prob, va)
            att = (acc[:, :PAIR] / acc[:, PAIR:]).astype(BF)
            out_ref[:, part, p * PAIR : (p + 1) * PAIR] = att.reshape(species, COLS, PAIR)


def column_attend(alive, mid, weights):
    species, columns, _ = mid.shape
    hd = weights.shape[1] // 3
    return pl.pallas_call(
        column_kernel,
        in_specs=[VMEM] * 3,
        out_specs=VMEM,
        out_shape=jax.ShapeDtypeStruct((species, columns, hd), BF),
        scratch_shapes=[pltpu.VMEM((3 * hd // PAIR, species, columns, PAIR), BF)],
        compiler_params=pltpu.CompilerParams(vmem_limit_bytes=24 * 2**20),
        name="column_attend",
    )(alive, mid, weights)


def last_kernel(mid_ref, att_ref, w_ref, out_ref):
    tile = out_ref.shape[0]
    part = pl.ds(pl.multiple_of(pl.program_id(0) * tile, tile), tile)
    out_ref[...] = (mid_ref[part] + dot(att_ref[part], w_ref[...])).astype(BF)


def last(mid, att, weights):
    rows, features = mid.shape
    tile = rows // 2
    return pl.pallas_call(
        last_kernel,
        grid=(rows // tile,),
        in_specs=[VMEM] * 3,
        out_specs=pl.BlockSpec((tile, features), lambda i: (i, 0)),
        out_shape=jax.ShapeDtypeStruct((rows, features), BF),
        compiler_params=pltpu.CompilerParams(vmem_limit_bytes=16 * 2**20),
        name="last",
    )(mid, att, weights)


def body(tokens, gap_mask, window_reach, row_qkv, row_out, col_qkv, col_out):
    _, blocklen, features = tokens.shape
    hd = row_out.shape[0]
    blocks = lax.axis_size("ctx")
    species = lax.axis_size("species")
    columns = blocklen // species
    near = [(i, i ^ 1) for i in range(blocks)]
    far = [(i, (i + 1 if i % 2 else i - 1) % blocks) for i in range(blocks)]
    x = tokens.reshape(blocklen, features)

    def by_column(array):
        return lax.all_to_all(array.reshape(species, columns, array.shape[1]), "species", 0, 0)

    x_far = lax.ppermute(x, "ctx", far)
    x, normed, wq, w_kv, own = keyval(x, row_qkv)
    fast = [lax.ppermute(kv, "ctx", near) for kv in own]
    q, mask, alive = queries(gap_mask, window_reach, normed, wq)
    acc, top = near_attend(mask, q, own, fast)
    mid, send = far_attend(mask, q, x_far, w_kv, acc, top, x, row_out)
    col_att = column_attend(alive, by_column(send), col_qkv)
    back = lax.all_to_all(col_att, "species", 0, 0)
    out = last(mid, back.reshape(blocklen, hd), col_out)
    return out.reshape(1, blocklen, features)


def solution(mesh):
    placed = (P("species", "ctx", None), P(), P(), P(), P(), P(), P())
    return jax.shard_map(
        body, mesh=mesh, in_specs=placed, out_specs=P("species", "ctx", None), check_vma=False
    )
```

```python
import math

import jax
import jax.numpy as jnp
from jax import lax
from jax.experimental import pallas as pl
from jax.experimental.pallas import tpu as pltpu
from jax.sharding import PartitionSpec as P

HEAD = 64
PAIR = 2 * HEAD
ROWS = 128
COLS = 16
NEAR = ((0, 1), (2, 3))
SCALE = HEAD ** (-0.5) / math.log(2.0)
BF = jnp.bfloat16
F32 = jnp.float32
VMEM = pl.BlockSpec(memory_space=pltpu.VMEM)
SMEM = pl.BlockSpec(memory_space=pltpu.SMEM)
HBM = pl.BlockSpec(memory_space=pltpu.HBM)


def dot(a, b):
    return jnp.dot(a, b, preferred_element_type=F32)


def dot_t(a, b):
    return lax.dot_general(a, b, (((1,), (1,)), ((), ())), preferred_element_type=F32)


def rms(values):
    return values * lax.rsqrt(jnp.mean(values * values, axis=-1, keepdims=True) + 1e-06)


def lower_half(rows):
    return lax.broadcasted_iota(jnp.int32, (rows, PAIR), 1) < HEAD


def one_head(pair, head):
    low = lower_half(pair.shape[0])
    keep = low if head == 0 else ~low
    return jnp.where(keep, pair, jnp.zeros_like(pair))


def values_and_ones(pair, head):
    return jnp.concatenate([one_head(pair, head), one_head(jnp.ones_like(pair), head)], axis=1)


def cost(flops, bytes_accessed):
    return pl.CostEstimate(flops=flops, bytes_accessed=bytes_accessed, transcendentals=0)


def window_of(gap_ref, reach_ref, blocklen, blocks, fast):
    block = lax.axis_index("ctx")
    species = lax.axis_index("species")
    odd = lax.rem(block, 2)
    before = odd == 1 if fast else odd == 0
    other = jnp.where(before, lax.rem(block + blocks - 1, blocks), lax.rem(block + 1, blocks))
    reach = reach_ref[block]
    low = jnp.where(before, blocklen - reach, 0)
    high = jnp.where(before, blocklen, reach)
    high = jnp.where(gap_ref[species, other] == 1, high, 0)
    cols = lax.broadcasted_iota(jnp.int32, (8, blocklen), 1)
    return jnp.where((cols >= low) & (cols < high), 1.0, 0.0)


def keyval_kernel(x_hbm, w_hbm, x_ref, n_ref, wq_ref, wk_ref, wv_ref, *refs):
    groups = NEAR
    kv_refs = refs[: len(groups)]
    xsem, wsem, qsem = refs[len(groups) :]
    rows = x_ref.shape[0]
    hd = wq_ref.shape[1]
    parts = xsem.shape[0]
    tile = rows // parts
    xs = [
        pltpu.make_async_copy(
            x_hbm.at[pl.ds(i * tile, tile)], x_ref.at[pl.ds(i * tile, tile)], xsem.at[i]
        )
        for i in range(parts)
    ]
    ws = [
        pltpu.make_async_copy(w_hbm.at[:, pl.ds(i * hd, hd)], w_ref, wsem.at[i - 1])
        for i, w_ref in ((1, wk_ref), (2, wv_ref))
    ]
    wq = pltpu.make_async_copy(w_hbm.at[:, pl.ds(0, hd)], wq_ref, qsem)
    for copy in xs + ws:
        copy.start()
    wq.start()
    for i in range(parts):
        xs[i].wait()
        part = pl.ds(i * tile, tile)
        n_ref[part] = rms(x_ref[part].astype(F32)).astype(BF)
    for copy in ws:
        copy.wait()
    keys = dot(n_ref[...], wk_ref[...]).astype(BF)
    values = dot(n_ref[...], wv_ref[...]).astype(BF)
    for kv_ref, group in zip(kv_refs, groups):
        for i, p in enumerate(group):
            kv_ref[i] = keys[:, p * PAIR : (p + 1) * PAIR]
            kv_ref[len(group) + i] = values[:, p * PAIR : (p + 1) * PAIR]
    wq.wait()


def keyval(x, weights):
    rows, features = x.shape
    hd = weights.shape[1] // 3
    out = pl.pallas_call(
        keyval_kernel,
        in_specs=[HBM] * 2,
        out_specs=[VMEM] * (5 + len(NEAR)),
        out_shape=[
            jax.ShapeDtypeStruct((rows, features), BF),
            jax.ShapeDtypeStruct((rows, features), BF),
            jax.ShapeDtypeStruct((features, hd), BF),
            jax.ShapeDtypeStruct((features, hd), BF),
            jax.ShapeDtypeStruct((features, hd), BF),
            *[jax.ShapeDtypeStruct((2 * len(group), rows, PAIR), BF) for group in NEAR],
        ],
        scratch_shapes=[
            pltpu.SemaphoreType.DMA((4,)),
            pltpu.SemaphoreType.DMA((2,)),
            pltpu.SemaphoreType.DMA,
        ],
        compiler_params=pltpu.CompilerParams(vmem_limit_bytes=47 * 2**20),
        cost_estimate=cost(1, 1),
        name="keyval",
    )(x, weights)
    return *out[:3], out[3:5], out[5:]


def query_kernel(gap_ref, reach_ref, n_ref, w_ref, q_ref, mask_ref, alive_ref):
    out = (dot(n_ref[...], w_ref[...]) * SCALE).astype(BF)
    for p in range(q_ref.shape[0]):
        q_ref[p] = out[:, p * PAIR : (p + 1) * PAIR]
    species, blocks = gap_ref.shape
    for i in range(2):
        mask_ref[i] = window_of(gap_ref, reach_ref, n_ref.shape[0], blocks, i == 0)
    lanes = lax.broadcasted_iota(jnp.int32, alive_ref.shape, 1)
    alive = jnp.zeros(alive_ref.shape, jnp.int32)
    for t in range(species):
        alive = jnp.where(lax.div(lanes, COLS) == t, gap_ref[t, lax.axis_index("ctx")], alive)
    alive_ref[...] = alive


def queries(gap_mask, reach, normed, weights):
    rows, features = normed.shape
    hd = weights.shape[1]
    species = gap_mask.shape[0]
    return pl.pallas_call(
        query_kernel,
        in_specs=[SMEM, SMEM, VMEM, VMEM],
        out_specs=[VMEM] * 3,
        out_shape=[
            jax.ShapeDtypeStruct((hd // PAIR, rows, PAIR), BF),
            jax.ShapeDtypeStruct((2, 8, rows), F32),
            jax.ShapeDtypeStruct((8, species * COLS), jnp.int32),
        ],
        compiler_params=pltpu.CompilerParams(vmem_limit_bytes=16 * 2**20),
        cost_estimate=cost(1, 1),
        name="queries",
    )(gap_mask, reach, normed, weights)


def near_kernel(mask_ref, q_ref, *refs):
    acc_ref, max_ref = refs[-2:]
    owns, fasts = refs[: len(NEAR)], refs[len(NEAR) : -2]
    pairs, rows, _ = q_ref.shape
    seen = mask_ref[0, :1] > 0.5

    def scores(p, t, keys_own, keys_fast):
        q = q_ref[p, pl.ds(t * ROWS, ROWS)]
        heads = [one_head(q, h) for h in range(2)]
        return [(dot_t(q, keys_own), dot_t(q, keys_fast)) for q in heads]

    def finish(p, t, found, va):
        part = pl.ds(t * ROWS, ROWS)
        probs = []
        for h, (so, sf) in enumerate(found):
            sf = jnp.where(seen, sf, -1e30)
            top = jnp.maximum(
                jnp.max(so, axis=-1, keepdims=True), jnp.max(sf, axis=-1, keepdims=True)
            )
            max_ref[2 * p + h, part] = jnp.broadcast_to(top, (ROWS, PAIR))
            probs += [jnp.exp2(so - top).astype(BF), jnp.exp2(sf - top).astype(BF)]
        acc_ref[p, part] = dot(jnp.concatenate(probs, axis=1), va)

    late = None
    for group, own, fast in zip(NEAR, owns, fasts):
        for i, p in enumerate(group):
            vals = (own[len(group) + i], fast[len(group) + i])
            va = jnp.concatenate([values_and_ones(v, h) for h in range(2) for v in vals], axis=0)
            for t in range(rows // ROWS):
                found = scores(p, t, own[i], fast[i])
                if late is not None:
                    finish(*late)
                late = (p, t, found, va)
    finish(*late)


def near_attend(mask, q, own, fast):
    pairs, rows, _ = q.shape
    return pl.pallas_call(
        near_kernel,
        in_specs=[VMEM] * (2 + 2 * len(NEAR)),
        out_specs=[VMEM, VMEM],
        out_shape=[
            jax.ShapeDtypeStruct((pairs, rows, 2 * PAIR), F32),
            jax.ShapeDtypeStruct((2 * pairs, rows, PAIR), F32),
        ],
        compiler_params=pltpu.CompilerParams(vmem_limit_bytes=24 * 2**20),
        cost_estimate=cost(1, 1),
        name="near_attend",
    )(mask, q, *own, *fast)


def far_kernel(mask_ref, q_ref, x_ref, wk_ref, wv_ref, acc_ref, max_ref, own_ref, wo_ref, mid_ref, send_ref, kv_ref, att_ref):
    pairs, rows, _ = q_ref.shape
    seen = mask_ref[1, :1] > 0.5
    normed = rms(x_ref[...].astype(F32)).astype(BF)
    for i, w_ref in enumerate((wk_ref, wv_ref)):
        out = dot(normed, w_ref[...]).astype(BF)
        for p in range(pairs):
            kv_ref[i * pairs + p] = out[:, p * PAIR : (p + 1) * PAIR]

    def scores(p, t):
        q = q_ref[p, pl.ds(t * ROWS, ROWS)]
        return [dot_t(one_head(q, h), kv_ref[p]) for h in range(2)]

    def finish(p, t, found, va):
        part = pl.ds(t * ROWS, ROWS)
        scales, probs = [], []
        for h, s in enumerate(found):
            s = jnp.where(seen, s, -1e30)
            before = max_ref[2 * p + h, part]
            top = jnp.maximum(jnp.max(s, axis=-1, keepdims=True), before)
            scales.append(jnp.exp2(before - top))
            probs.append(jnp.exp2(s - jnp.concatenate([top] * (rows // PAIR), axis=1)).astype(BF))
        acc = dot(jnp.concatenate(probs, axis=1), va)
        scale = jnp.where(lower_half(ROWS), scales[0], scales[1])
        old = acc_ref[p, part]
        num = acc[:, :PAIR] + old[:, :PAIR] * scale
        den = acc[:, PAIR:] + old[:, PAIR:] * scale
        att_ref[part, p * PAIR : (p + 1) * PAIR] = (num / den).astype(BF)

    late = None
    for p in range(pairs):
        va = jnp.concatenate([values_and_ones(kv_ref[pairs + p], h) for h in range(2)], axis=0)
        for t in range(rows // ROWS):
            found = scores(p, t)
            if late is not None:
                finish(*late)
            late = (p, t, found, va)
    finish(*late)
    mid = own_ref[...].astype(F32) + dot(att_ref[...], wo_ref[...])
    mid_ref[...] = mid
    send_ref[...] = mid.astype(BF)


def far_attend(mask, q, x_far, w_kv, acc, top, x, w_out):
    pairs, rows, _ = q.shape
    features = x.shape[1]
    return pl.pallas_call(
        far_kernel,
        in_specs=[VMEM] * 9,
        out_specs=[VMEM] * 2,
        out_shape=[
            jax.ShapeDtypeStruct((rows, features), F32),
            jax.ShapeDtypeStruct((rows, features), BF),
        ],
        scratch_shapes=[
            pltpu.VMEM((2 * pairs, rows, PAIR), BF),
            pltpu.VMEM((rows, pairs * PAIR), BF),
        ],
        compiler_params=pltpu.CompilerParams(vmem_limit_bytes=24 * 2**20),
        cost_estimate=cost(6 * 10**9, 2**23),
        name="far_attend",
    )(mask, q, x_far, *w_kv, acc, top, x, w_out)


def column_kernel(alive_ref, mid_ref, w_ref, out_ref, pack_ref):
    species, columns, features = mid_ref.shape
    hd = out_ref.shape[2]
    pairs = hd // PAIR
    n = rms(mid_ref[...].reshape(species * columns, features).astype(F32)).astype(BF)
    for j in range(3):
        out = dot(n, w_ref[:, j * hd : (j + 1) * hd])
        if j == 0:
            out = out * SCALE
        out = out.astype(BF).reshape(species, columns, hd)
        for p in range(pairs):
            pack_ref[j * pairs + p] = out[:, :, p * PAIR : (p + 1) * PAIR]
    rows = species * COLS
    qrow = lax.broadcasted_iota(jnp.int32, (rows, rows), 0)
    krow = lax.broadcasted_iota(jnp.int32, (rows, rows), 1)
    seen = (lax.rem(qrow, COLS) == lax.rem(krow, COLS)) & (alive_ref[:1] == 1)
    seen = jnp.concatenate([seen, seen], axis=0)
    for j in range(columns // COLS):
        part = pl.ds(j * COLS, COLS)
        for p in range(pairs):
            q = pack_ref[p, :, part, :].reshape(rows, PAIR)
            k = pack_ref[pairs + p, :, part, :].reshape(rows, PAIR)
            v = pack_ref[2 * pairs + p, :, part, :].reshape(rows, PAIR)
            qs = jnp.concatenate([one_head(q, 0), one_head(q, 1)], axis=0)
            s = jnp.where(seen, dot_t(qs, k), -1e30)
            prob = jnp.exp2(s - jnp.max(s, axis=-1, keepdims=True)).astype(BF)
            prob = jnp.concatenate([prob[:rows], prob[rows:]], axis=1)
            va = jnp.concatenate([values_and_ones(v, 0), values_and_ones(v, 1)], axis=0)
            acc = dot(prob, va)
            att = (acc[:, :PAIR] / acc[:, PAIR:]).astype(BF)
            out_ref[:, part, p * PAIR : (p + 1) * PAIR] = att.reshape(species, COLS, PAIR)


def column_attend(alive, mid, weights):
    species, columns, _ = mid.shape
    hd = weights.shape[1] // 3
    return pl.pallas_call(
        column_kernel,
        in_specs=[VMEM] * 3,
        out_specs=VMEM,
        out_shape=jax.ShapeDtypeStruct((species, columns, hd), BF),
        scratch_shapes=[pltpu.VMEM((3 * hd // PAIR, species, columns, PAIR), BF)],
        compiler_params=pltpu.CompilerParams(vmem_limit_bytes=24 * 2**20),
        name="column_attend",
    )(alive, mid, weights)


def last_kernel(mid_ref, att_ref, w_ref, out_ref):
    tile = out_ref.shape[0]
    part = pl.ds(pl.multiple_of(pl.program_id(0) * tile, tile), tile)
    out_ref[...] = (mid_ref[part] + dot(att_ref[part], w_ref[...])).astype(BF)


def last(mid, att, weights):
    rows, features = mid.shape
    tile = rows // 2
    return pl.pallas_call(
        last_kernel,
        grid=(rows // tile,),
        in_specs=[VMEM] * 3,
        out_specs=pl.BlockSpec((tile, features), lambda i: (i, 0)),
        out_shape=jax.ShapeDtypeStruct((rows, features), BF),
        compiler_params=pltpu.CompilerParams(vmem_limit_bytes=16 * 2**20),
        name="last",
    )(mid, att, weights)


def body(tokens, gap_mask, window_reach, row_qkv, row_out, col_qkv, col_out):
    _, blocklen, features = tokens.shape
    hd = row_out.shape[0]
    blocks = lax.axis_size("ctx")
    species = lax.axis_size("species")
    columns = blocklen // species
    near = [(i, i ^ 1) for i in range(blocks)]
    far = [(i, (i + 1 if i % 2 else i - 1) % blocks) for i in range(blocks)]
    x = tokens.reshape(blocklen, features)

    def by_column(array):
        return lax.all_to_all(array.reshape(species, columns, array.shape[1]), "species", 0, 0)

    x_far = lax.ppermute(x, "ctx", far)
    x, normed, wq, w_kv, own = keyval(x, row_qkv)
    fast = [lax.ppermute(kv, "ctx", near) for kv in own]
    q, mask, alive = queries(gap_mask, window_reach, normed, wq)
    acc, top = near_attend(mask, q, own, fast)
    mid, send = far_attend(mask, q, x_far, w_kv, acc, top, x, row_out)
    col_att = column_attend(alive, by_column(send), col_qkv)
    back = lax.all_to_all(col_att, "species", 0, 0)
    out = last(mid, back.reshape(blocklen, hd), col_out)
    return out.reshape(1, blocklen, features)


def solution(mesh):
    placed = (P("species", "ctx", None), P(), P(), P(), P(), P(), P())
    return jax.shard_map(
        body, mesh=mesh, in_specs=placed, out_specs=P("species", "ctx", None), check_vma=False
    )
```

```python
import math

import jax
import jax.numpy as jnp
from jax import lax
from jax.experimental import pallas as pl
from jax.experimental.pallas import tpu as pltpu
from jax.sharding import PartitionSpec as P

HEAD = 64
PAIR = 2 * HEAD
ROWS = 128
COLS = 16
NEAR = ((0, 1), (2, 3))
SCALE = HEAD ** (-0.5) / math.log(2.0)
BF = jnp.bfloat16
F32 = jnp.float32
VMEM = pl.BlockSpec(memory_space=pltpu.VMEM)
SMEM = pl.BlockSpec(memory_space=pltpu.SMEM)
HBM = pl.BlockSpec(memory_space=pltpu.HBM)


def dot(a, b):
    return jnp.dot(a, b, preferred_element_type=F32)


def dot_t(a, b):
    return lax.dot_general(a, b, (((1,), (1,)), ((), ())), preferred_element_type=F32)


def rms(values):
    return values * lax.rsqrt(jnp.mean(values * values, axis=-1, keepdims=True) + 1e-06)


def lower_half(rows):
    return lax.broadcasted_iota(jnp.int32, (rows, PAIR), 1) < HEAD


def one_head(pair, head):
    low = lower_half(pair.shape[0])
    keep = low if head == 0 else ~low
    return jnp.where(keep, pair, jnp.zeros_like(pair))


def values_and_ones(pair, head):
    return jnp.concatenate([one_head(pair, head), one_head(jnp.ones_like(pair), head)], axis=1)


def cost(flops, bytes_accessed):
    return pl.CostEstimate(flops=flops, bytes_accessed=bytes_accessed, transcendentals=0)


def window_of(gap_ref, reach_ref, blocklen, blocks, fast):
    block = lax.axis_index("ctx")
    species = lax.axis_index("species")
    odd = lax.rem(block, 2)
    before = odd == 1 if fast else odd == 0
    other = jnp.where(before, lax.rem(block + blocks - 1, blocks), lax.rem(block + 1, blocks))
    reach = reach_ref[block]
    low = jnp.where(before, blocklen - reach, 0)
    high = jnp.where(before, blocklen, reach)
    high = jnp.where(gap_ref[species, other] == 1, high, 0)
    cols = lax.broadcasted_iota(jnp.int32, (8, blocklen), 1)
    return jnp.where((cols >= low) & (cols < high), 1.0, 0.0)


def keyval_kernel(x_hbm, w_hbm, x_ref, n_ref, wq_ref, wk_ref, wv_ref, *refs):
    groups = NEAR
    kv_refs = refs[: len(groups)]
    xsem, wsem, qsem = refs[len(groups) :]
    rows = x_ref.shape[0]
    hd = wq_ref.shape[1]
    parts = xsem.shape[0]
    tile = rows // parts
    xs = [
        pltpu.make_async_copy(
            x_hbm.at[pl.ds(i * tile, tile)], x_ref.at[pl.ds(i * tile, tile)], xsem.at[i]
        )
        for i in range(parts)
    ]
    ws = [
        pltpu.make_async_copy(w_hbm.at[:, pl.ds(i * hd, hd)], w_ref, wsem.at[i - 1])
        for i, w_ref in ((1, wk_ref), (2, wv_ref))
    ]
    wq = pltpu.make_async_copy(w_hbm.at[:, pl.ds(0, hd)], wq_ref, qsem)
    for copy in xs + ws:
        copy.start()
    wq.start()
    for i in range(parts):
        xs[i].wait()
        part = pl.ds(i * tile, tile)
        n_ref[part] = rms(x_ref[part].astype(F32)).astype(BF)
    for copy in ws:
        copy.wait()
    keys = dot(n_ref[...], wk_ref[...]).astype(BF)
    values = dot(n_ref[...], wv_ref[...]).astype(BF)
    for kv_ref, group in zip(kv_refs, groups):
        for i, p in enumerate(group):
            kv_ref[i] = keys[:, p * PAIR : (p + 1) * PAIR]
            kv_ref[len(group) + i] = values[:, p * PAIR : (p + 1) * PAIR]
    wq.wait()


def keyval(x, weights):
    rows, features = x.shape
    hd = weights.shape[1] // 3
    out = pl.pallas_call(
        keyval_kernel,
        in_specs=[HBM] * 2,
        out_specs=[VMEM] * (5 + len(NEAR)),
        out_shape=[
            jax.ShapeDtypeStruct((rows, features), BF),
            jax.ShapeDtypeStruct((rows, features), BF),
            jax.ShapeDtypeStruct((features, hd), BF),
            jax.ShapeDtypeStruct((features, hd), BF),
            jax.ShapeDtypeStruct((features, hd), BF),
            *[jax.ShapeDtypeStruct((2 * len(group), rows, PAIR), BF) for group in NEAR],
        ],
        scratch_shapes=[
            pltpu.SemaphoreType.DMA((4,)),
            pltpu.SemaphoreType.DMA((2,)),
            pltpu.SemaphoreType.DMA,
        ],
        compiler_params=pltpu.CompilerParams(vmem_limit_bytes=47 * 2**20),
        cost_estimate=cost(1, 1),
        name="keyval",
    )(x, weights)
    return *out[:3], out[3:5], out[5:]


def query_kernel(gap_ref, reach_ref, n_ref, w_ref, q_ref, mask_ref, alive_ref):
    out = (dot(n_ref[...], w_ref[...]) * SCALE).astype(BF)
    for p in range(q_ref.shape[0]):
        q_ref[p] = out[:, p * PAIR : (p + 1) * PAIR]
    species, blocks = gap_ref.shape
    for i in range(2):
        mask_ref[i] = window_of(gap_ref, reach_ref, n_ref.shape[0], blocks, i == 0)
    lanes = lax.broadcasted_iota(jnp.int32, alive_ref.shape, 1)
    alive = jnp.zeros(alive_ref.shape, jnp.int32)
    for t in range(species):
        alive = jnp.where(lax.div(lanes, COLS) == t, gap_ref[t, lax.axis_index("ctx")], alive)
    alive_ref[...] = alive


def queries(gap_mask, reach, normed, weights):
    rows, features = normed.shape
    hd = weights.shape[1]
    species = gap_mask.shape[0]
    return pl.pallas_call(
        query_kernel,
        in_specs=[SMEM, SMEM, VMEM, VMEM],
        out_specs=[VMEM] * 3,
        out_shape=[
            jax.ShapeDtypeStruct((hd // PAIR, rows, PAIR), BF),
            jax.ShapeDtypeStruct((2, 8, rows), F32),
            jax.ShapeDtypeStruct((8, species * COLS), jnp.int32),
        ],
        compiler_params=pltpu.CompilerParams(vmem_limit_bytes=16 * 2**20),
        cost_estimate=cost(1, 1),
        name="queries",
    )(gap_mask, reach, normed, weights)


def near_kernel(mask_ref, q_ref, *refs):
    acc_ref, max_ref = refs[-2:]
    owns, fasts = refs[: len(NEAR)], refs[len(NEAR) : -2]
    pairs, rows, _ = q_ref.shape
    seen = mask_ref[0, :1] > 0.5

    def scores(p, t, keys_own, keys_fast):
        q = q_ref[p, pl.ds(t * ROWS, ROWS)]
        heads = [one_head(q, h) for h in range(2)]
        return [(dot_t(q, keys_own), dot_t(q, keys_fast)) for q in heads]

    def finish(p, t, found, va):
        part = pl.ds(t * ROWS, ROWS)
        probs = []
        for h, (so, sf) in enumerate(found):
            sf = jnp.where(seen, sf, -1e30)
            top = jnp.maximum(
                jnp.max(so, axis=-1, keepdims=True), jnp.max(sf, axis=-1, keepdims=True)
            )
            max_ref[2 * p + h, part] = jnp.broadcast_to(top, (ROWS, PAIR))
            probs += [jnp.exp2(so - top).astype(BF), jnp.exp2(sf - top).astype(BF)]
        acc_ref[p, part] = dot(jnp.concatenate(probs, axis=1), va)

    late = None
    for group, own, fast in zip(NEAR, owns, fasts):
        for i, p in enumerate(group):
            vals = (own[len(group) + i], fast[len(group) + i])
            va = jnp.concatenate([values_and_ones(v, h) for h in range(2) for v in vals], axis=0)
            for t in range(rows // ROWS):
                found = scores(p, t, own[i], fast[i])
                if late is not None:
                    finish(*late)
                late = (p, t, found, va)
    finish(*late)


def near_attend(mask, q, own, fast):
    pairs, rows, _ = q.shape
    return pl.pallas_call(
        near_kernel,
        in_specs=[VMEM] * (2 + 2 * len(NEAR)),
        out_specs=[VMEM, VMEM],
        out_shape=[
            jax.ShapeDtypeStruct((pairs, rows, 2 * PAIR), F32),
            jax.ShapeDtypeStruct((2 * pairs, rows, PAIR), F32),
        ],
        compiler_params=pltpu.CompilerParams(vmem_limit_bytes=24 * 2**20),
        cost_estimate=cost(1, 1),
        name="near_attend",
    )(mask, q, *own, *fast)


def far_kernel(mask_ref, q_ref, x_ref, wk_ref, wv_ref, acc_ref, max_ref, own_ref, wo_ref, mid_ref, send_ref, kv_ref, att_ref):
    pairs, rows, _ = q_ref.shape
    seen = mask_ref[1, :1] > 0.5
    normed = rms(x_ref[...].astype(F32)).astype(BF)
    for i, w_ref in enumerate((wk_ref, wv_ref)):
        out = dot(normed, w_ref[...]).astype(BF)
        for p in range(pairs):
            kv_ref[i * pairs + p] = out[:, p * PAIR : (p + 1) * PAIR]

    def scores(p, t):
        q = q_ref[p, pl.ds(t * ROWS, ROWS)]
        return [dot_t(one_head(q, h), kv_ref[p]) for h in range(2)]

    def finish(p, t, found, va):
        part = pl.ds(t * ROWS, ROWS)
        scales, probs = [], []
        for h, s in enumerate(found):
            s = jnp.where(seen, s, -1e30)
            before = max_ref[2 * p + h, part]
            top = jnp.maximum(jnp.max(s, axis=-1, keepdims=True), before)
            scales.append(jnp.exp2(before - top))
            probs.append(jnp.exp2(s - jnp.concatenate([top] * (rows // PAIR), axis=1)).astype(BF))
        acc = dot(jnp.concatenate(probs, axis=1), va)
        scale = jnp.where(lower_half(ROWS), scales[0], scales[1])
        old = acc_ref[p, part]
        num = acc[:, :PAIR] + old[:, :PAIR] * scale
        den = acc[:, PAIR:] + old[:, PAIR:] * scale
        att_ref[part, p * PAIR : (p + 1) * PAIR] = (num / den).astype(BF)

    late = None
    for p in range(pairs):
        va = jnp.concatenate([values_and_ones(kv_ref[pairs + p], h) for h in range(2)], axis=0)
        for t in range(rows // ROWS):
            found = scores(p, t)
            if late is not None:
                finish(*late)
            late = (p, t, found, va)
    finish(*late)
    mid = own_ref[...].astype(F32) + dot(att_ref[...], wo_ref[...])
    mid_ref[...] = mid
    send_ref[...] = mid.astype(BF)


def far_attend(mask, q, x_far, w_kv, acc, top, x, w_out):
    pairs, rows, _ = q.shape
    features = x.shape[1]
    return pl.pallas_call(
        far_kernel,
        in_specs=[VMEM] * 9,
        out_specs=[VMEM] * 2,
        out_shape=[
            jax.ShapeDtypeStruct((rows, features), F32),
            jax.ShapeDtypeStruct((rows, features), BF),
        ],
        scratch_shapes=[
            pltpu.VMEM((2 * pairs, rows, PAIR), BF),
            pltpu.VMEM((rows, pairs * PAIR), BF),
        ],
        compiler_params=pltpu.CompilerParams(vmem_limit_bytes=24 * 2**20),
        cost_estimate=cost(6 * 10**9, 2**23),
        name="far_attend",
    )(mask, q, x_far, *w_kv, acc, top, x, w_out)


def column_kernel(alive_ref, mid_ref, w_ref, out_ref, pack_ref):
    species, columns, features = mid_ref.shape
    hd = out_ref.shape[2]
    pairs = hd // PAIR
    half = columns // 2

    def normed(place):
        part = mid_ref[:, place * half : (place + 1) * half, :]
        return rms(part.reshape(species * half, features).astype(F32)).astype(BF)

    def project(n, place, j):
        out = dot(n, w_ref[:, j * hd : (j + 1) * hd])
        if j == 0:
            out = out * SCALE
        out = out.astype(BF).reshape(species, half, hd)
        for p in range(pairs):
            pack_ref[j * pairs + p, :, pl.ds(place * half, half), :] = out[
                :, :, p * PAIR : (p + 1) * PAIR
            ]

    rows = species * COLS
    qrow = lax.broadcasted_iota(jnp.int32, (rows, rows), 0)
    krow = lax.broadcasted_iota(jnp.int32, (rows, rows), 1)
    seen = (lax.rem(qrow, COLS) == lax.rem(krow, COLS)) & (alive_ref[:1] == 1)
    seen = jnp.concatenate([seen, seen], axis=0)

    def attend(j, p):
        part = pl.ds(j * COLS, COLS)
        q = pack_ref[p, :, part, :].reshape(rows, PAIR)
        k = pack_ref[pairs + p, :, part, :].reshape(rows, PAIR)
        v = pack_ref[2 * pairs + p, :, part, :].reshape(rows, PAIR)
        qs = jnp.concatenate([one_head(q, 0), one_head(q, 1)], axis=0)
        s = jnp.where(seen, dot_t(qs, k), -1e30)
        prob = jnp.exp2(s - jnp.max(s, axis=-1, keepdims=True)).astype(BF)
        prob = jnp.concatenate([prob[:rows], prob[rows:]], axis=1)
        va = jnp.concatenate([values_and_ones(v, 0), values_and_ones(v, 1)], axis=0)
        acc = dot(prob, va)
        att = (acc[:, :PAIR] / acc[:, PAIR:]).astype(BF)
        out_ref[:, part, p * PAIR : (p + 1) * PAIR] = att.reshape(species, COLS, PAIR)

    items = [(j, p) for j in range(columns // COLS) for p in range(pairs)]
    early, late = items[: len(items) // 2], items[len(items) // 2 :]
    first, second = normed(0), normed(1)
    for j in range(3):
        project(first, 0, j)
    for j in range(3):
        project(second, 1, j)
        for item in early[j * len(early) // 3 : (j + 1) * len(early) // 3]:
            attend(*item)
    for item in late:
        attend(*item)


def column_attend(alive, mid, weights):
    species, columns, _ = mid.shape
    hd = weights.shape[1] // 3
    return pl.pallas_call(
        column_kernel,
        in_specs=[VMEM] * 3,
        out_specs=VMEM,
        out_shape=jax.ShapeDtypeStruct((species, columns, hd), BF),
        scratch_shapes=[pltpu.VMEM((3 * hd // PAIR, species, columns, PAIR), BF)],
        compiler_params=pltpu.CompilerParams(vmem_limit_bytes=24 * 2**20),
        name="column_attend",
    )(alive, mid, weights)


def last_kernel(mid_ref, att_ref, w_ref, out_ref):
    tile = out_ref.shape[0]
    part = pl.ds(pl.multiple_of(pl.program_id(0) * tile, tile), tile)
    out_ref[...] = (mid_ref[part] + dot(att_ref[part], w_ref[...])).astype(BF)


def last(mid, att, weights):
    rows, features = mid.shape
    tile = rows // 2
    return pl.pallas_call(
        last_kernel,
        grid=(rows // tile,),
        in_specs=[VMEM] * 3,
        out_specs=pl.BlockSpec((tile, features), lambda i: (i, 0)),
        out_shape=jax.ShapeDtypeStruct((rows, features), BF),
        compiler_params=pltpu.CompilerParams(vmem_limit_bytes=16 * 2**20),
        name="last",
    )(mid, att, weights)


def body(tokens, gap_mask, window_reach, row_qkv, row_out, col_qkv, col_out):
    _, blocklen, features = tokens.shape
    hd = row_out.shape[0]
    blocks = lax.axis_size("ctx")
    species = lax.axis_size("species")
    columns = blocklen // species
    near = [(i, i ^ 1) for i in range(blocks)]
    far = [(i, (i + 1 if i % 2 else i - 1) % blocks) for i in range(blocks)]
    x = tokens.reshape(blocklen, features)

    def by_column(array):
        return lax.all_to_all(array.reshape(species, columns, array.shape[1]), "species", 0, 0)

    x_far = lax.ppermute(x, "ctx", far)
    x, normed, wq, w_kv, own = keyval(x, row_qkv)
    fast = [lax.ppermute(kv, "ctx", near) for kv in own]
    q, mask, alive = queries(gap_mask, window_reach, normed, wq)
    acc, top = near_attend(mask, q, own, fast)
    mid, send = far_attend(mask, q, x_far, w_kv, acc, top, x, row_out)
    col_att = column_attend(alive, by_column(send), col_qkv)
    back = lax.all_to_all(col_att, "species", 0, 0)
    out = last(mid, back.reshape(blocklen, hd), col_out)
    return out.reshape(1, blocklen, features)


def solution(mesh):
    placed = (P("species", "ctx", None), P(), P(), P(), P(), P(), P())
    return jax.shard_map(
        body, mesh=mesh, in_specs=placed, out_specs=P("species", "ctx", None), check_vma=False
    )
```
